128 devices in a mesh: dp: 4 (over y_hi, core), expert: 8 (over y_lo, z), etp: 4 (over x).
Axes of the slice: x: 4, y: 4 (y_hi: 2, y_lo: 2; y = y_hi * 2 + y_lo), z: 4, core: 2. Of those that a mesh axis runs over, the one named last changes fastest.
Arguments:
- layer_input: bfloat16 [4096, 3072], P(('dp', 'expert'), 'etp'), may hold values from -6 to 6
- grad_output: bfloat16 [4096, 3072], P(('dp', 'expert'), 'etp'), may hold values from -6 to 6
- expert_ids: int32 [4096, 2], P(('dp', 'expert')), may hold values from 0 to 7, all different within a row; in each aligned block of 128 rows (0 to 127, 128 to 255, ...) at most 36 rows name the same one
- gate_probs: float32 [4096, 2], P(('dp', 'expert')), may hold values from 0.1 to 1
- up_weight: bfloat16 [8, 3072, 16384], P('expert', None, ('dp', 'etp')), may hold values from -0.15625 to 0.15625
- down_weight: bfloat16 [8, 16384, 3072], P('expert', ('dp', 'etp')), may hold values from -0.046875 to 0.046875
Outputs:
- grad_input: bfloat16 [4096, 3072], P(('dp', 'expert'), 'etp')
- grad_up: bfloat16 [8, 3072, 16384], P('expert', None, ('dp', 'etp'))
- grad_down: bfloat16 [8, 16384, 3072], P('expert', ('dp', 'etp'))
The draws below stay inside these ranges and needn't reach their ends.
Inputs may be any that keep to these rules, and one draw needn't show every extreme that they name: `expert_ids`: among the 128 tokens of one index of dp+expert (aligned blocks of rows) no expert is named more than 36 times, a bound that some block reaches; the two picks of a token differ.
All inputs are finite; a program needn't handle non-finite values.
Results may differ from the reference program's by a relative error of at most 0.02.
Values may be sent and summed in bfloat16 or wider, within the bound.
A program may use at most 192 MiB of HBM per device.

```python
import math
import jax
import jax.numpy as jnp
import numpy as np
from jax import lax

D = 3072
FF = 16384
TOK_GRP = 128
EXPERTS = 8
TOKENS = 4096
CAP = 36
N_DP = 4
N_ETP = 4


def strengthened(values, rng, source, target, shards_of, factor):
    def block_of(dim):
        return (jnp.arange(values.shape[dim]) // (values.shape[dim] // shards_of)).reshape((-1,) + (1,) * (values.ndim - 1 - dim))

    first = jax.random.permutation(rng, shards_of)[block_of(target)]
    other_side = (block_of(target) + shards_of // 2) % shards_of
    return jnp.where((block_of(source) == first) | (block_of(source) == other_side), factor * values, values)


def shard_levels(rng, extent, pieces, least, high):
    loudness = 1.0
    for dim, shards_of in pieces:
        draws = jax.random.uniform(jax.random.fold_in(jax.random.fold_in(rng, 6), dim), (shards_of,), jnp.float32, least / len(pieces), high / len(pieces))
        loudness = loudness * jnp.repeat(jnp.exp(draws), extent[dim] // shards_of).reshape((-1,) + (1,) * (len(extent) - 1 - dim))
    return loudness


def deal_out(stream_key, own, number, rows, number_of, top, most, lean):
    sequence = jax.random.permutation(stream_key, number_of)
    heavy_load, ordinary = load_shares(number_of, rows * top, most, lean, True), load_shares(number_of, rows * top, most, lean, False)
    places = jnp.arange(number_of)

    def named(sizes, offset_by):
        used = int((sizes > 0).sum())
        fixed = max(1, used // 4)
        moved = fixed + (places - fixed + offset_by * (used - fixed)) % max(1, number_of - fixed)
        return jnp.zeros((number_of,), jnp.int32).at[sequence[jnp.where(places < fixed, places, moved)]].set(jnp.asarray(sizes, jnp.int32))

    sizes = jnp.where(number % 4 == 0, named(heavy_load, number // 4), named(ordinary, number - number // 4 - 1))
    mixed = jax.random.permutation(jax.random.fold_in(own, 3), number_of)
    donor, taker = mixed[0:number_of // 2 * 2:2], mixed[1:number_of // 2 * 2:2]
    margin = jnp.minimum(sizes[donor] - 1, most - sizes[taker]) // 2
    margin = jnp.where((donor == sequence[0]) | (taker == sequence[0]) | (sizes[taker] == 0), 0, jnp.maximum(margin, 0))
    moved = jax.random.randint(jax.random.fold_in(own, 4), (number_of // 2,), 0, 1 << 20) % (margin + 1)
    sizes = sizes.at[donor].add(-moved).at[taker].add(moved)
    members = jnp.searchsorted(jnp.cumsum(sizes), jnp.arange(rows * top), side="right").astype(jnp.int32)
    listing = members.reshape(top, rows).T
    listing = listing[jax.random.permutation(jax.random.fold_in(own, 1), rows)]
    offset_by = jax.random.randint(jax.random.fold_in(own, 2), (rows, 1), 0, top)
    return jnp.take_along_axis(listing, (jnp.arange(top)[None, :] + offset_by) % top, axis=1)


def load_shares(number_of, total, reach, lean, full):
    weights = [(1 << 20) // math.isqrt(grade ** lean) + 1 for grade in range(1, number_of + 1)]
    largest = reach if full else min(reach, max(-(-total // number_of), total * weights[0] // sum(weights)))
    least = 1 if total - largest >= number_of - 1 else 0
    counts, surplus = [largest] + [least] * (number_of - 1), total - largest - least * (number_of - 1)
    while surplus > 0:
        movable = [i for i in range(1, number_of) if counts[i] < largest] or [i for i in range(1, number_of) if counts[i] < reach]
        pool, budget = sum([weights[i] for i in movable]), surplus
        for i in movable:
            more = min(reach - counts[i], max(1, budget * weights[i] // pool), surplus)
            counts[i] = counts[i] + more
            surplus = surplus - more
    return np.array(counts)


def centred(stream_key, extent, spread, most, pieces=(), kind=jnp.bfloat16):
    drawn = spread * jax.random.normal(stream_key, extent, jnp.float32)
    if pieces:
        drawn = drawn * shard_levels(stream_key, extent, pieces, -0.22, 0.18)
    return jnp.clip(drawn, -most, most).astype(kind)


def gaussian_with(rng, extent, deviation, bound, split, heavy, held_as=jnp.bfloat16):
    drawn = deviation * jax.random.normal(rng, extent, jnp.float32)
    if split:
        drawn = drawn * shard_levels(rng, extent, split, -0.22, 0.18)
    return jnp.clip(strengthened(drawn, jax.random.fold_in(rng, 3), *heavy), -bound, bound).astype(held_as)


def setup_inputs(seed: int = 0) -> dict:
    key_of = jax.random.split(jax.random.key(seed), 7)
    layer_input = centred(key_of[0], (TOKENS, D), 1.0, 6.0, ((0, 32), (1, 4)))
    grad_output = centred(key_of[1], (TOKENS, D), 1.0, 6.0, ((0, 32), (1, 4)))
    expert_ids_keys = jax.random.split(jax.random.fold_in(key_of[2], 1), TOKENS // TOK_GRP)
    expert_ids_turns = jax.random.permutation(jax.random.fold_in(key_of[2], 3), TOKENS // TOK_GRP)
    expert_ids = jax.vmap(lambda own, number: deal_out(jax.random.fold_in(key_of[2], 2), own, number, TOK_GRP, EXPERTS, 2, CAP, 2))(expert_ids_keys, expert_ids_turns).reshape((TOKENS, 2))
    gate_probs = jnp.clip(0.1 + 0.9 * jax.random.uniform(key_of[3], (TOKENS, 2), jnp.float32) ** shard_levels(key_of[3], (TOKENS, 2), ((0, 32),), -0.2, 0.2), 0.1, 1.0)
    up_weight = gaussian_with(key_of[4], (EXPERTS, D, FF), D ** -0.5, 0.15625, ((0, 8), (2, 16)), (2, 1, 16, 2.0))
    down_weight = centred(key_of[5], (EXPERTS, FF, D), FF ** -0.5, 0.046875, ((0, 8), (1, 16)))
    return {"layer_input": layer_input, "grad_output": grad_output, "expert_ids": expert_ids, "gate_probs": gate_probs, "up_weight": up_weight, "down_weight": down_weight}


inv_root_two = 0.7071067811865476
inv_root_tau = 0.3989422804014327


def gelu_value(value):
    return 0.5 * value * (1.0 + lax.erf(value * inv_root_two))


def gelu_slope(value):
    return 0.5 * (1.0 + lax.erf(value * inv_root_two)) + value * jnp.exp(-0.5 * value * value) * inv_root_tau


def slot_table(routes, experts, capacity):
    flat_ids = routes.reshape(-1)
    onehot = (flat_ids[:, None] == jnp.arange(experts, dtype=jnp.int32)[None, :]).astype(jnp.int32)
    before = jnp.cumsum(onehot, axis=0) - onehot
    position = jnp.sum(before * onehot, axis=1)
    return (flat_ids * capacity + position).astype(jnp.int32)


def expert_block(rows_x, rows_g, up_block, down_block):
    before_act = jnp.dot(rows_x, up_block, preferred_element_type=jnp.float32)
    hidden = gelu_value(before_act).astype(jnp.bfloat16)
    back_grad = lax.dot_general(rows_g, down_block, (((1,), (1,)), ((), ())), preferred_element_type=jnp.float32)
    pre_grad = (back_grad * gelu_slope(before_act)).astype(jnp.bfloat16)
    down_part = lax.dot_general(hidden, rows_g, (((0,), (0,)), ((), ())), preferred_element_type=jnp.float32)
    up_part = lax.dot_general(rows_x, pre_grad, (((0,), (0,)), ((), ())), preferred_element_type=jnp.float32)
    return pre_grad, up_part, down_part


def reference(layer_input, grad_output, expert_ids, gate_probs, up_weight, down_weight):
    groups = TOKENS // TOK_GRP
    rows_all = groups * CAP
    group_routes = expert_ids.reshape(groups, TOK_GRP, 2)
    slots = jax.vmap(lambda group_ids: slot_table(group_ids, EXPERTS, CAP))(group_routes)
    expert_of = slots // CAP
    row_of = (jnp.arange(groups, dtype=jnp.int32)[:, None] * CAP + slots % CAP).astype(jnp.int32)
    scaled = (grad_output.astype(jnp.float32)[:, None, :] * gate_probs[:, :, None]).astype(jnp.bfloat16)
    scaled = scaled.reshape(groups, 2 * TOK_GRP, D)
    doubled = jnp.repeat(layer_input, 2, axis=0).reshape(groups, 2 * TOK_GRP, D)
    blank_rows = jnp.zeros((EXPERTS, rows_all, D), jnp.bfloat16)
    buf_x = blank_rows.at[expert_of, row_of].set(doubled)
    buf_g = blank_rows.at[expert_of, row_of].set(scaled)
    blocks = N_DP * N_ETP
    block_width = FF // blocks

    def per_expert(operands):
        rows_x, rows_g, up_one, down_one = operands
        up_blocks = up_one.reshape(D, blocks, block_width).transpose(1, 0, 2)
        down_blocks = down_one.reshape(blocks, block_width, D)

        def step(running, pair):
            up_block, down_block = pair
            pre_grad, up_part, down_part = expert_block(rows_x, rows_g, up_block, down_block)
            slice_part = lax.dot_general(pre_grad, up_block, (((1,), (1,)), ((), ())), preferred_element_type=jnp.float32).astype(jnp.bfloat16)
            slice_part = lax.optimization_barrier(slice_part)
            running = running + slice_part.astype(jnp.float32)
            return running, (up_part.astype(jnp.bfloat16), down_part.astype(jnp.bfloat16))

        running, (up_parts, down_parts) = lax.scan(step, jnp.zeros((rows_all, D), jnp.float32), (up_blocks, down_blocks))
        return running, up_parts.transpose(1, 0, 2).reshape(D, FF), down_parts.reshape(FF, D)

    input_rows, grad_up, grad_down = lax.map(per_expert, (buf_x, buf_g, up_weight, down_weight))
    picked = input_rows[expert_of, row_of].reshape(groups, TOK_GRP, 2, D)
    grad_input = jnp.sum(picked, axis=2).reshape(TOKENS, D).astype(jnp.bfloat16)
    return grad_input, grad_up, grad_down
```

```python
import jax
import jax.numpy as jnp
from jax import lax
from jax.experimental import pallas as pl
from jax.experimental.pallas import tpu as pltpu
from jax.sharding import PartitionSpec as P

inv_root_two = 0.7071067811865476
inv_root_tau = 0.3989422804014327
MESH = pl.DeviceIdType.MESH
bf16 = jnp.bfloat16
f32 = jnp.float32

TOK = 128
QUARTER = 768
CAP = 36
BLOCK = 4 * CAP
CHUNK = 2 * BLOCK
ROWS = 4 * CHUNK
D = 3072
F = 1024
TILE = 256
HALF = QUARTER // 2
OFFSETS = (0, 3, 1, 2)
N_SEMS = 80


def kernel(
    x_ref, g_ref, meta_ref, up_hbm, down_hbm,
    gi_ref, gup_hbm, gdown_hbm,
    rows_x, rows_g, up, down, hid, pre, dense_x, dense_g, meta, place, pk_x, pk_g,
    dx, r1, r2a, r2b, zret, yd, y1, y2,
    ssem, rsem, wsem, osem,
):
    dp = lax.axis_index("dp")
    ex = lax.axis_index("expert")
    x = lax.axis_index("etp")
    c = dp % 2
    yl = ex // 4
    z = ex % 4
    y = (dp // 2) * 2 + yl

    def device(x_, y_, z_, c_):
        return ((y_ // 2) * 2 + c_, (y_ % 2) * 4 + z_, x_)

    xp, xm, xo = (x + 1) % 4, (x + 3) % 4, (x + 2) % 4
    yp, ym, yo = (y + 1) % 4, (y + 3) % 4, (y + 2) % 4
    to_xp, to_xm = device(xp, y, z, c), device(xm, y, z, c)
    to_yp, to_ym = device(x, yp, z, c), device(x, ym, z, c)
    to_core = device(x, y, z, 1 - c)
    to_z = {d: device(x, y, (z + d) % 4, c) for d in (1, 2, 3)}

    sent = []

    def send(src, dst, to):
        i = len(sent)
        copy = pltpu.make_async_remote_copy(
            src_ref=src, dst_ref=dst, send_sem=ssem.at[i], recv_sem=rsem.at[i],
            device_id=to, device_id_type=MESH,
        )
        copy.start()
        sent.append(copy)
        return copy

    load_up = pltpu.make_async_copy(up_hbm.at[0], up, wsem.at[0])
    load_down = pltpu.make_async_copy(down_hbm.at[0], down, wsem.at[1])
    load_up.start()
    load_down.start()

    partners = (to_xp, to_xm, to_yp, to_ym, to_core, to_z[1], to_z[2], to_z[3])
    barrier = pltpu.get_barrier_semaphore()
    for partner in partners:
        pl.semaphore_signal(barrier, inc=1, device_id=partner, device_id_type=MESH)
    pl.semaphore_wait(barrier, len(partners))

    def tok(y_):
        return pl.ds(pl.multiple_of(y_ * TOK, TOK), TOK)

    a_xp = send(x_ref, dense_x.at[tok(y)], to_yp)
    a_mp = send(meta_ref, meta.at[y], to_yp)
    a_gm = send(g_ref, dense_g.at[tok(y)], to_ym)
    a_mm = send(meta_ref, meta.at[y], to_ym)
    a_xm = send(x_ref, dense_x.at[tok(y)], to_ym)
    a_gp = send(g_ref, dense_g.at[tok(y)], to_yp)
    dense_x[tok(y), :] = x_ref[...]
    dense_g[tok(y), :] = g_ref[...]
    meta[y] = meta_ref[...]
    a_xp.wait_recv()
    b_x = send(dense_x.at[tok(ym)], dense_x.at[tok(ym)], to_yp)
    a_mp.wait_recv()
    b_m = send(meta.at[ym], meta.at[ym], to_yp)
    a_gm.wait_recv()
    b_g = send(dense_g.at[tok(yp)], dense_g.at[tok(yp)], to_ym)
    for copy in (a_mm, b_m):
        copy.wait_recv()

    row = lax.broadcasted_iota(jnp.int32, (4 * BLOCK, TOK), 0).astype(f32)
    gate = jnp.zeros((4 * BLOCK, 1), f32)
    for t in range(4):
        m = meta[t]
        first = row == jnp.where(yl == 0, m[0:1], m[2:3])
        second = row == jnp.where(yl == 0, m[1:2], m[3:4])
        hits = jnp.where(first, 1.0, 0.0) + jnp.where(second, 1.0, 0.0)
        place[:, t * TOK:(t + 1) * TOK] = hits.astype(bf16)
        gates = jnp.where(first, m[4:5], 0.0) + jnp.where(second, m[5:6], 0.0)
        gate = gate + jnp.sum(gates, axis=1, keepdims=True)
    for copy in (a_xm, a_gp, b_x, b_g):
        copy.wait_recv()
    pk_x[...] = jnp.dot(place[...], dense_x[...], preferred_element_type=f32).astype(bf16)
    pk_g[...] = (jnp.dot(place[...], dense_g[...], preferred_element_type=f32) * gate).astype(bf16)

    def packed(z_):
        return pl.ds(pl.multiple_of(z_ * BLOCK, BLOCK), BLOCK)

    def block(z_, c_):
        return pl.ds(pl.multiple_of((z_ * 2 + c_) * BLOCK, BLOCK), BLOCK)

    def chunk(z_):
        return pl.ds(pl.multiple_of(z_ * CHUNK, CHUNK), CHUNK)

    def part(x_):
        return pl.ds(pl.multiple_of(x_ * QUARTER, QUARTER), QUARTER)

    z_in = {}
    for d in (1, 3, 2):
        there = packed((z + d) % 4)
        here = (block(z, c), part(x))
        z_in[d] = (
            send(pk_x.at[there], rows_x.at[here], to_z[d]),
            send(pk_g.at[there], rows_g.at[here], to_z[d]),
        )
    rows_x[block(z, c), part(x)] = pk_x[packed(z), :]
    rows_g[block(z, c), part(x)] = pk_g[packed(z), :]

    zs = [(z + o) % 4 for o in OFFSETS]
    x_in = {}
    fwd = {}
    c_in = {}
    r1_in = {}
    r2a_in = {}
    r2b_in = {}
    rz_in = []

    def x_send(j):
        if j > 0:
            for copy in z_in[(4 - OFFSETS[j]) % 4]:
                copy.wait_recv()
        at = (block(zs[j], c), part(x))
        x_in[j] = (
            send(rows_x.at[at], rows_x.at[at], to_xp),
            send(rows_g.at[at], rows_g.at[at], to_xm),
            send(rows_x.at[at], rows_x.at[at], to_xm),
            send(rows_g.at[at], rows_g.at[at], to_xp),
        )

    def x_forward(j):
        x_in[j][0].wait_recv()
        at = (block(zs[j], c), part(xm))
        one = send(rows_x.at[at], rows_x.at[at], to_xp)
        x_in[j][1].wait_recv()
        at = (block(zs[j], c), part(xp))
        two = send(rows_g.at[at], rows_g.at[at], to_xm)
        fwd[j] = (one, two)

    def core_send(j):
        for copy in (x_in[j][2], x_in[j][3]) + fwd[j]:
            copy.wait_recv()
        at = block(zs[j], c)
        c_in[j] = (
            send(rows_x.at[at], rows_x.at[at], to_core),
            send(rows_g.at[at], rows_g.at[at], to_core),
        )

    def hidden_of(j):
        for copy in c_in[j]:
            copy.wait_recv()
        rows = chunk(zs[j])

        @pl.loop(0, F // TILE)
        def _(n):
            cols = pl.ds(pl.multiple_of(n * TILE, TILE), TILE)
            act = jnp.dot(rows_x[rows, :], up[:, cols], preferred_element_type=f32)
            back = lax.dot_general(
                rows_g[rows, :], down[cols, :], (((1,), (1,)), ((), ())),
                preferred_element_type=f32,
            )
            half_cdf = 0.5 * (1.0 + lax.erf(act * inv_root_two))
            hid[rows, cols] = (act * half_cdf).astype(bf16)
            slope = half_cdf + act * jnp.exp(-0.5 * act * act) * inv_root_tau
            pre[rows, cols] = (back * slope).astype(bf16)

    def input_grad_of(j):
        rows = chunk(zs[j])

        @pl.loop(0, D // TILE)
        def _(n):
            cols = pl.ds(pl.multiple_of(n * TILE, TILE), TILE)
            dx[rows, cols] = lax.dot_general(
                pre[rows, :], up[cols, :], (((1,), (1,)), ((), ())),
                preferred_element_type=f32,
            ).astype(bf16)

        r1_in[j] = send(dx.at[block(zs[j], 1 - c)], r1.at[j], to_core)

    def add_core(j):
        r1_in[j].wait_recv()
        rows = block(zs[j], c)
        dx[rows, :] = (dx[rows, :].astype(f32) + r1[j].astype(f32)).astype(bf16)
        start = pl.multiple_of(xo * QUARTER, HALF)
        r2a_in[j] = (
            send(dx.at[rows, pl.ds(start, HALF)], r2a.at[j, 0], to_xp),
            send(dx.at[rows, pl.ds(pl.multiple_of(start + HALF, HALF), HALF)], r2a.at[j, 1], to_xm),
        )

    def add_far(j):
        rows = block(zs[j], c)
        r2a_in[j][0].wait_recv()
        cols = pl.ds(pl.multiple_of(xp * QUARTER, HALF), HALF)
        dx[rows, cols] = (dx[rows, cols].astype(f32) + r2a[j, 0].astype(f32)).astype(bf16)
        one = send(dx.at[rows, part(xp)], r2b.at[j, 0], to_xp)
        r2a_in[j][1].wait_recv()
        cols = pl.ds(pl.multiple_of(xm * QUARTER + HALF, HALF), HALF)
        dx[rows, cols] = (dx[rows, cols].astype(f32) + r2a[j, 1].astype(f32)).astype(bf16)
        two = send(dx.at[rows, part(xm)], r2b.at[j, 1], to_xm)
        r2b_in[j] = (one, two)

    def add_near(j):
        rows = block(zs[j], c)
        for copy in r2b_in[j]:
            copy.wait_recv()
        total = (
            dx[rows, part(x)].astype(f32) + r2b[j, 0].astype(f32) + r2b[j, 1].astype(f32)
        ).astype(bf16)
        if OFFSETS[j] == 0:
            zret[packed(z), :] = total
        else:
            dx[rows, part(x)] = total
            rz_in.append(
                send(dx.at[rows, part(x)], zret.at[packed(z)], to_z[OFFSETS[j]])
            )

    stores = []

    def down_tiles(first, last):
        @pl.loop(first, last)
        def _(n):
            cols = pl.ds(pl.multiple_of(n * TILE, TILE), TILE)
            for k in range(D // F):
                wide = slice(k * F, (k + 1) * F)
                down[cols, wide] = lax.dot_general(
                    hid[:, cols], rows_g[:, wide], (((0,), (0,)), ((), ())),
                    preferred_element_type=f32,
                ).astype(bf16)

        rows = slice(first * TILE, last * TILE)
        store = pltpu.make_async_copy(down.at[rows], gdown_hbm.at[0, rows], osem.at[len(stores)])
        store.start()
        stores.append(store)

    def up_tiles(first, last):
        @pl.loop(first, last)
        def _(n):
            cols = pl.ds(pl.multiple_of(n * TILE, TILE), TILE)
            up[cols, :] = lax.dot_general(
                rows_x[:, cols], pre[...], (((0,), (0,)), ((), ())),
                preferred_element_type=f32,
            ).astype(bf16)

        rows = slice(first * TILE, last * TILE)
        store = pltpu.make_async_copy(up.at[rows], gup_hbm.at[0, rows], osem.at[len(stores)])
        store.start()
        stores.append(store)

    x_send(0)
    x_send(1)
    load_up.wait()
    load_down.wait()
    x_forward(0)
    core_send(0)
    x_send(2)
    hidden_of(0)
    x_forward(1)
    input_grad_of(0)
    core_send(1)
    x_send(3)
    hidden_of(1)
    x_forward(2)
    add_core(0)
    input_grad_of(1)
    core_send(2)
    add_far(0)
    hidden_of(2)
    x_forward(3)
    add_near(0)
    add_core(1)
    input_grad_of(2)
    core_send(3)
    add_far(1)
    hidden_of(3)
    add_near(1)
    add_core(2)
    input_grad_of(3)
    add_far(2)
    down_tiles(0, 1)
    add_near(2)
    add_core(3)
    down_tiles(1, 2)
    add_far(3)
    down_tiles(2, 4)
    add_near(3)
    up_tiles(0, 4)

    for copy in rz_in:
        copy.wait_recv()
    yd[...] = lax.dot_general(
        place[...], zret[...], (((0,), (0,)), ((), ())), preferred_element_type=f32
    ).astype(bf16)
    low, high = slice(0, HALF), slice(HALF, QUARTER)
    y1_in = (
        send(yd.at[tok(yo), low], y1.at[0], to_yp),
        send(yd.at[tok(yo), high], y1.at[1], to_ym),
    )
    up_tiles(4, 8)
    y1_in[0].wait_recv()
    yd[tok(yp), low] = (yd[tok(yp), low].astype(f32) + y1[0].astype(f32)).astype(bf16)
    y2_p = send(yd.at[tok(yp)], y2.at[0], to_yp)
    y1_in[1].wait_recv()
    yd[tok(ym), high] = (yd[tok(ym), high].astype(f32) + y1[1].astype(f32)).astype(bf16)
    y2_m = send(yd.at[tok(ym)], y2.at[1], to_ym)
    up_tiles(8, 12)
    y2_p.wait_recv()
    y2_m.wait_recv()
    gi_ref[...] = (
        yd[tok(y), :].astype(f32) + y2[0].astype(f32) + y2[1].astype(f32)
    ).astype(bf16)
    for copy in sent:
        copy.wait_send()
    for store in stores:
        store.wait()


def on_device(layer_input, grad_output, expert_ids, gate_probs, up_weight, down_weight):
    dp = lax.axis_index("dp")
    ex = lax.axis_index("expert")
    y = (dp // 2) * 2 + ex // 4
    flat = expert_ids.T.reshape(-1)
    order = jnp.arange(2 * TOK, dtype=jnp.int32)
    same = (flat[:, None] == flat[None, :]) & (order[:, None] < order[None, :])
    position = jnp.sum(same.astype(jnp.int32), axis=0)
    target = ((flat % 4) * BLOCK + y * CAP + position).astype(f32).reshape(2, TOK)
    parity = (flat // 4).reshape(2, TOK)
    meta = jnp.concatenate(
        [
            jnp.where(parity == 0, target, -1.0),
            jnp.where(parity == 1, target, -1.0),
            gate_probs.T,
            jnp.zeros((2, TOK), f32),
        ],
        axis=0,
    )
    vmem = pl.BlockSpec(memory_space=pltpu.VMEM)
    hbm = pl.BlockSpec(memory_space=pl.ANY)
    return pl.pallas_call(
        kernel,
        out_shape=(
            jax.ShapeDtypeStruct((TOK, QUARTER), bf16),
            jax.ShapeDtypeStruct(up_weight.shape, bf16),
            jax.ShapeDtypeStruct(down_weight.shape, bf16),
        ),
        in_specs=[vmem, vmem, vmem, hbm, hbm],
        out_specs=(vmem, hbm, hbm),
        scratch_shapes=[
            pltpu.VMEM((ROWS, D), bf16),
            pltpu.VMEM((ROWS, D), bf16),
            pltpu.VMEM((D, F), bf16),
            pltpu.VMEM((F, D), bf16),
            pltpu.VMEM((ROWS, F), bf16),
            pltpu.VMEM((ROWS, F), bf16),
            pltpu.VMEM((4 * TOK, QUARTER), bf16),
            pltpu.VMEM((4 * TOK, QUARTER), bf16),
            pltpu.VMEM((4, 8, TOK), f32),
            pltpu.VMEM((4 * BLOCK, 4 * TOK), bf16),
            pltpu.VMEM((4 * BLOCK, QUARTER), bf16),
            pltpu.VMEM((4 * BLOCK, QUARTER), bf16),
            pltpu.VMEM((ROWS, D), bf16),
            pltpu.VMEM((4, BLOCK, D), bf16),
            pltpu.VMEM((4, 2, BLOCK, HALF), bf16),
            pltpu.VMEM((4, 2, BLOCK, QUARTER), bf16),
            pltpu.VMEM((4 * BLOCK, QUARTER), bf16),
            pltpu.VMEM((4 * TOK, QUARTER), bf16),
            pltpu.VMEM((2, TOK, HALF), bf16),
            pltpu.VMEM((2, TOK, QUARTER), bf16),
            pltpu.SemaphoreType.DMA((N_SEMS,)),
            pltpu.SemaphoreType.DMA((N_SEMS,)),
            pltpu.SemaphoreType.DMA((2,)),
            pltpu.SemaphoreType.DMA((8,)),
        ],
        compiler_params=pltpu.CompilerParams(
            collective_id=0, has_side_effects=True, vmem_limit_bytes=63 * 1024 * 1024
        ),
    )(layer_input, grad_output, meta, up_weight, down_weight)


def solution(mesh):
    return jax.shard_map(
        on_device,
        mesh=mesh,
        in_specs=(
            P(("dp", "expert"), "etp"),
            P(("dp", "expert"), "etp"),
            P(("dp", "expert"), None),
            P(("dp", "expert"), None),
            P("expert", None, ("dp", "etp")),
            P("expert", ("dp", "etp"), None),
        ),
        out_specs=(
            P(("dp", "expert"), "etp"),
            P("expert", None, ("dp", "etp")),
            P("expert", ("dp", "etp"), None),
        ),
        check_vma=False,
    )
```

```python
import jax
import jax.numpy as jnp
from jax import lax
from jax.experimental import pallas as pl
from jax.experimental.pallas import tpu as pltpu
from jax.sharding import PartitionSpec as P

inv_root_two = 0.7071067811865476
inv_root_tau = 0.3989422804014327
MESH = pl.DeviceIdType.MESH
bf16 = jnp.bfloat16
f32 = jnp.float32

TOK = 128
QUARTER = 768
NEAR = 512
FAR = 256
CAP = 36
BLOCK = 4 * CAP
CHUNK = 2 * BLOCK
ROWS = 4 * CHUNK
D = 3072
F = 1024
SPLIT = 4 * NEAR
ALL_FAR = 4 * FAR
TILE = 256
WIDE = 512
FAR_PARTS = (pl.ds(0, ALL_FAR // 2), pl.ds(ALL_FAR // 2, ALL_FAR // 2))
OFFSETS = (0, 3, 1, 2)
N_SEMS = 142
SEND_SEMS = 48


def pieces():
    out = []
    for k in range(4):
        out.append((k * NEAR, k * QUARTER, NEAR))
        out.append((SPLIT + k * FAR, k * QUARTER + NEAR, FAR))
    return out


def kernel(
    x_ref, g_ref, ids_ref, gates_ref, up_hbm, down_hbm,
    gi_ref, gup_hbm, gdown_hbm,
    rows_x, rows_g, up, down, hid, pre, meta, place,
    d1x, d1g, d2x, d2g, p1x, p1g, p2x, p2g,
    dx, r1, r2a, r2b, z1, z2, yd1, yd2, y1a, y1b, y2a, y2b, xsum, xa, xb,
    ssem, rsem, wsem, osem,
):
    dp = lax.axis_index("dp")
    ex = lax.axis_index("expert")
    x = lax.axis_index("etp")
    c = dp % 2
    yl = ex // 4
    z = ex % 4
    y = (dp // 2) * 2 + yl

    def device(x_, y_, z_, c_):
        return ((y_ // 2) * 2 + c_, (y_ % 2) * 4 + z_, x_)

    xp, xm, xo = (x + 1) % 4, (x + 3) % 4, (x + 2) % 4
    yp, ym, yo = (y + 1) % 4, (y + 3) % 4, (y + 2) % 4
    to_xp, to_xm = device(xp, y, z, c), device(xm, y, z, c)
    to_yp, to_ym = device(x, yp, z, c), device(x, ym, z, c)
    to_core = device(x, y, z, 1 - c)
    to_z = {d: device(x, y, (z + d) % 4, c) for d in (1, 2, 3)}

    def span(start, width):
        return pl.ds(pl.multiple_of(start, width), width)

    def tok(y_):
        return span(y_ * TOK, TOK)

    def packed(z_):
        return span(z_ * BLOCK, BLOCK)

    def block(z_, c_):
        return span((z_ * 2 + c_) * BLOCK, BLOCK)

    def chunk(z_):
        return span(z_ * CHUNK, CHUNK)

    def near(x_):
        return span(x_ * NEAR, NEAR)

    def far(x_):
        return span(x_ * FAR, FAR)

    all_near, all_far = slice(0, SPLIT), slice(SPLIT, D)
    sent = []

    def send(src, dst, to):
        i = len(sent)
        if i >= SEND_SEMS:
            sent[i - SEND_SEMS].wait_send()
        copy = pltpu.make_async_remote_copy(
            src_ref=src, dst_ref=dst, send_sem=ssem.at[i % SEND_SEMS], recv_sem=rsem.at[i],
            device_id=to, device_id_type=MESH,
        )
        copy.start()
        sent.append(copy)
        return copy

    def arrived(copies):
        for copy in copies:
            copy.wait_recv()

    def gather(own, into, below, here, above, down_to, up_to):
        one, two = into
        first = (
            send(own[0], one(here), up_to),
            send(own[1], two(here), down_to),
            send(own[0], one(here), down_to),
            send(own[1], two(here), up_to),
        )

        def forward():
            first[0].wait_recv()
            up = send(one(below), one(below), up_to)
            first[1].wait_recv()
            down = send(two(above), two(above), down_to)
            return (first[2], first[3], up, down)

        return forward

    def scatter(at, half, below, here, above, opposite, down_to, up_to, a, b):
        low, high = slice(0, half), slice(half, 2 * half)
        halves = (send(at(opposite, low), a.at[0], up_to), send(at(opposite, high), a.at[1], down_to))

        def middle():
            halves[0].wait_recv()
            ref = at(above, low)
            ref[...] = (ref[...].astype(f32) + a[0].astype(f32)).astype(bf16)
            up = send(at(above, None), b.at[0], up_to)
            halves[1].wait_recv()
            ref = at(below, high)
            ref[...] = (ref[...].astype(f32) + a[1].astype(f32)).astype(bf16)
            down = send(at(below, None), b.at[1], down_to)

            def end():
                arrived((up, down))
                return at(here, None)[...].astype(f32) + b[0].astype(f32) + b[1].astype(f32)

            return end

        return middle

    partners = (to_xp, to_xm, to_yp, to_ym, to_core, to_z[1], to_z[2], to_z[3])
    barrier = pltpu.get_barrier_semaphore()
    for partner in partners:
        pl.semaphore_signal(barrier, inc=1, device_id=partner, device_id_type=MESH)
    pl.semaphore_wait(barrier, len(partners))

    lo, hi = pl.ds(0, NEAR), pl.ds(NEAR, FAR)
    y1_forward = gather(
        (x_ref.at[:, lo], g_ref.at[:, lo]),
        (lambda k: d1x.at[tok(k)], lambda k: d1g.at[tok(k)]),
        ym, y, yp, to_ym, to_yp,
    )
    x2_forward = gather(
        (x_ref.at[:, hi], g_ref.at[:, hi]),
        (lambda k: d2x.at[tok(y), far(k)], lambda k: d2g.at[tok(y), far(k)]),
        xm, x, xp, to_xm, to_xp,
    )
    for there, here, width in pieces():
        pltpu.make_async_copy(
            up_hbm.at[0, pl.ds(here, width), :], up.at[pl.ds(there, width), :], wsem.at[0]
        ).start()
        pltpu.make_async_copy(
            down_hbm.at[0, :, pl.ds(here, width)], down.at[:, pl.ds(there, width)], wsem.at[1]
        ).start()

    ids = ids_ref[...]
    expert = lax.broadcasted_iota(jnp.int32, (8, TOK), 0)
    one = jnp.where(expert == ids[0:1], 1.0, 0.0)
    two = jnp.where(expert == ids[1:2], 1.0, 0.0)
    earlier = (
        lax.broadcasted_iota(jnp.int32, (TOK, TOK), 0) < lax.broadcasted_iota(jnp.int32, (TOK, TOK), 1)
    )
    before = jnp.dot(
        jnp.concatenate([one, two], axis=0).astype(bf16),
        jnp.where(earlier, 1.0, 0.0).astype(bf16),
        preferred_element_type=f32,
    )
    one_at = jnp.sum(before[:8] * one, axis=0, keepdims=True)
    two_at = jnp.sum((before[8:] + jnp.sum(one, axis=1, keepdims=True)) * two, axis=0, keepdims=True)
    upper = ids >= 4
    base = (jnp.where(upper, ids - 4, ids) * BLOCK + y * CAP).astype(f32)
    for k, at in ((0, one_at), (1, two_at)):
        target = base[k:k + 1] + at
        meta[y, k:k + 1] = jnp.where(upper[k:k + 1], -1.0, target)
        meta[y, k + 2:k + 3] = jnp.where(upper[k:k + 1], target, -1.0)
        meta[y, k + 4:k + 5] = gates_ref[k:k + 1, :]
    meta[y, 6:8] = jnp.zeros((2, TOK), f32)
    m_p = send(meta.at[y], meta.at[y], to_yp)
    m_m = send(meta.at[y], meta.at[y], to_ym)
    d1x[tok(y), :] = x_ref[:, lo]
    d1g[tok(y), :] = g_ref[:, lo]
    d2x[tok(y), far(x)] = x_ref[:, hi]
    d2g[tok(y), far(x)] = g_ref[:, hi]

    x2_in = x2_forward()
    y1_in = y1_forward()
    m_p.wait_recv()
    m_f = send(meta.at[ym], meta.at[ym], to_yp)
    arrived(x2_in)

    def y2_gather(cols):
        return gather(
            (d2x.at[tok(y), cols], d2g.at[tok(y), cols]),
            (lambda k: d2x.at[tok(k), cols], lambda k: d2g.at[tok(k), cols]),
            ym, y, yp, to_ym, to_yp,
        )

    y2_forward = [y2_gather(FAR_PARTS[0])]
    arrived((m_m, m_f))
    row = lax.broadcasted_iota(jnp.int32, (4 * BLOCK, TOK), 0).astype(f32)
    gate = jnp.zeros((4 * BLOCK, 1), f32)
    for t in range(4):
        m = meta[t]
        first = row == jnp.where(yl == 0, m[0:1], m[2:3])
        second = row == jnp.where(yl == 0, m[1:2], m[3:4])
        hits = jnp.where(first, 1.0, 0.0) + jnp.where(second, 1.0, 0.0)
        place[:, t * TOK:(t + 1) * TOK] = hits.astype(bf16)
        gates = jnp.where(first, m[4:5], 0.0) + jnp.where(second, m[5:6], 0.0)
        gate = gate + jnp.sum(gates, axis=1, keepdims=True)

    def pack(from_x, from_g, to_x, to_g, cols):
        to_x[:, cols] = jnp.dot(place[...], from_x[:, cols], preferred_element_type=f32).astype(bf16)
        to_g[:, cols] = (
            jnp.dot(place[...], from_g[:, cols], preferred_element_type=f32) * gate
        ).astype(bf16)

    def to_expert(d, from_x, from_g, cols, into):
        there = (packed((z + d) % 4), cols)
        here = (block(z, c), into)
        return (
            send(from_x.at[there], rows_x.at[here], to_z[d]),
            send(from_g.at[there], rows_g.at[here], to_z[d]),
        )

    def keep(from_x, from_g, cols, into):
        here = (block(z, c), into)
        rows_x[here] = from_x[packed(z), cols]
        rows_g[here] = from_g[packed(z), cols]

    zs = [(z + o) % 4 for o in OFFSETS]
    x_in = {}
    near_z = {}
    far_z = {}
    near_in = {}
    far_in = {}
    r1_far = {}
    r1_near = {}
    r2_middle = {}
    r2_end = {}
    z1_in = []
    z2_in = []

    def x_send(j):
        if j > 0:
            arrived(near_z[(4 - OFFSETS[j]) % 4])
        rows = block(zs[j], c)
        x_in[j] = gather(
            (rows_x.at[rows, near(x)], rows_g.at[rows, near(x)]),
            (lambda k: rows_x.at[rows, near(k)], lambda k: rows_g.at[rows, near(k)]),
            xm, x, xp, to_xm, to_xp,
        )

    def x_forward(j):
        x_in[j] = x_in[j]()

    def near_send(j):
        arrived(x_in[j])
        at = (block(zs[j], c), all_near)
        near_in[j] = [send(r.at[at], r.at[at], to_core) for r in (rows_x, rows_g)]

    def far_send(j):
        if j > 0:
            arrived(far_z[(4 - OFFSETS[j]) % 4])
        at = (block(zs[j], c), all_far)
        far_in[j] = [send(r.at[at], r.at[at], to_core) for r in (rows_x, rows_g)]

    def hidden_of(j):
        arrived(near_in[j])
        arrived(far_in[j])
        rows = chunk(zs[j])

        @pl.loop(0, F // WIDE)
        def _(n):
            cols = pl.ds(pl.multiple_of(n * WIDE, WIDE), WIDE)
            act = jnp.dot(rows_x[rows, :], up[:, cols], preferred_element_type=f32)
            back = lax.dot_general(
                rows_g[rows, :], down[cols, :], (((1,), (1,)), ((), ())),
                preferred_element_type=f32,
            )
            half_cdf = 0.5 * (1.0 + lax.erf(act * inv_root_two))
            hid[rows, cols] = (act * half_cdf).astype(bf16)
            slope = half_cdf + act * jnp.exp(-0.5 * act * act) * inv_root_tau
            pre[rows, cols] = (back * slope).astype(bf16)

    def input_grad(j, first, last):
        rows = chunk(zs[j])

        @pl.loop(first, last)
        def _(n):
            cols = pl.ds(pl.multiple_of(n * F, F), F)
            dx[rows, cols] = lax.dot_general(
                pre[rows, :], up[cols, :], (((1,), (1,)), ((), ())),
                preferred_element_type=f32,
            ).astype(bf16)

    def input_grad_of(j):
        input_grad(j, SPLIT // F, D // F)
        r1_far[j] = send(dx.at[block(zs[j], 1 - c), all_far], r1.at[j, :, all_far], to_core)
        input_grad(j, 0, SPLIT // F)
        r1_near[j] = send(dx.at[block(zs[j], 1 - c), all_near], r1.at[j, :, all_near], to_core)

    def add_core(j):
        rows = block(zs[j], c)
        r1_far[j].wait_recv()
        total = (dx[rows, all_far].astype(f32) + r1[j, :, all_far].astype(f32)).astype(bf16)
        if OFFSETS[j] == 0:
            z2[packed(z), :] = total
        else:
            dx[rows, all_far] = total
            z2_in.append(send(dx.at[rows, all_far], z2.at[packed(z)], to_z[OFFSETS[j]]))
        r1_near[j].wait_recv()
        dx[rows, all_near] = (
            dx[rows, all_near].astype(f32) + r1[j, :, all_near].astype(f32)
        ).astype(bf16)

        def at(k, half):
            if half is None:
                return dx.at[rows, near(k)]
            return dx.at[rows, span(k * NEAR + half.start, NEAR // 2)]

        r2_middle[j] = scatter(at, NEAR // 2, xm, x, xp, xo, to_xm, to_xp, r2a.at[j], r2b.at[j])

    def add_far(j):
        r2_end[j] = r2_middle[j]()

    def add_near(j):
        rows = block(zs[j], c)
        total = r2_end[j]().astype(bf16)
        if OFFSETS[j] == 0:
            z1[packed(z), :] = total
        else:
            dx[rows, near(x)] = total
            z1_in.append(send(dx.at[rows, near(x)], z1.at[packed(z)], to_z[OFFSETS[j]]))

    def unpack(rows, tokens):
        tokens[...] = lax.dot_general(
            place[...], rows[...], (((0,), (0,)), ((), ())), preferred_element_type=f32
        ).astype(bf16)

    def over_x(tokens, a, b):
        def at(k, part):
            return tokens.at[:, far(k)] if part is None else tokens.at[:, span(k * FAR + part.start, FAR // 2)]

        return scatter(at, FAR // 2, xm, x, xp, xo, to_xm, to_xp, a, b)

    def over_y(tokens, half, a, b):
        def at(k, part):
            return tokens.at[tok(k)] if part is None else tokens.at[tok(k), part]

        return scatter(at, half, ym, y, yp, yo, to_ym, to_yp, a, b)

    def down_tiles(first, last):
        @pl.loop(first, last)
        def _(u):
            cols = pl.ds(pl.multiple_of(u // 3 * TILE, TILE), TILE)
            wide = pl.ds(pl.multiple_of(u % 3 * F, F), F)
            down[cols, wide] = lax.dot_general(
                hid[:, cols], rows_g[:, wide], (((0,), (0,)), ((), ())),
                preferred_element_type=f32,
            ).astype(bf16)

        for n in range(first // 3, last // 3):
            rows = pl.ds(n * TILE, TILE)
            for there, here, width in pieces():
                pltpu.make_async_copy(
                    down.at[rows, pl.ds(there, width)], gdown_hbm.at[0, rows, pl.ds(here, width)], osem.at[1]
                ).start()

    def up_tiles(first, last):
        @pl.loop(first, last)
        def _(n):
            cols = pl.ds(pl.multiple_of(n * TILE, TILE), TILE)
            up[cols, :] = lax.dot_general(
                rows_x[:, cols], pre[...], (((0,), (0,)), ((), ())),
                preferred_element_type=f32,
            ).astype(bf16)

        for there, here, width in pieces():
            for t in range(0, width, TILE):
                if first * TILE <= there + t < last * TILE:
                    pltpu.make_async_copy(
                        up.at[pl.ds(there + t, TILE)], gup_hbm.at[0, pl.ds(here + t, TILE)], osem.at[0]
                    ).start()

    def near_to(d):
        near_z[d] = to_expert(d, p1x, p1g, pl.ds(0, NEAR), near(x))

    def far_to(d, part):
        into = pl.ds(SPLIT + part * (ALL_FAR // 2), ALL_FAR // 2)
        far_z[d] = far_z.get(d, ()) + to_expert(d, p2x, p2g, FAR_PARTS[part], into)

    def far_pack(part):
        pack(d2x, d2g, p2x, p2g, FAR_PARTS[part])
        far_to(1, part)
        far_to(3, part)
        keep(p2x, p2g, FAR_PARTS[part], pl.ds(SPLIT + part * (ALL_FAR // 2), ALL_FAR // 2))

    arrived(y1_in)
    pack(d1x, d1g, p1x, p1g, pl.ds(0, NEAR))
    near_to(1)
    near_to(3)
    keep(p1x, p1g, pl.ds(0, NEAR), near(x))
    x_send(0)
    y2_first = y2_forward[0]()
    y2_second = y2_gather(FAR_PARTS[1])
    x_send(1)
    near_to(2)
    x_forward(0)
    arrived(y2_first)
    far_pack(0)
    x_send(2)
    y2_second = y2_second()
    x_forward(1)
    arrived(y2_second)
    far_pack(1)
    near_send(0)
    far_send(0)
    far_to(2, 0)
    far_to(2, 1)
    x_send(3)
    pltpu.make_async_copy(up_hbm.at[0], up, wsem.at[0]).wait()
    pltpu.make_async_copy(down_hbm.at[0], down, wsem.at[1]).wait()
    hidden_of(0)
    x_forward(2)
    near_send(1)
    input_grad_of(0)
    far_send(1)
    x_forward(3)
    add_core(0)
    near_send(2)
    hidden_of(1)
    far_send(2)
    add_far(0)
    input_grad_of(1)
    near_send(3)
    add_core(1)
    hidden_of(2)
    far_send(3)
    add_near(0)
    add_far(1)
    input_grad_of(2)
    add_core(2)
    add_near(1)
    hidden_of(3)
    add_far(2)
    input_grad_of(3)
    add_near(2)
    down_tiles(0, 2)
    add_core(3)
    down_tiles(2, 5)
    add_far(3)
    down_tiles(5, 8)
    add_near(3)
    arrived(z2_in)
    unpack(z2, yd2)
    x_middle = over_x(yd2, xa, xb)
    down_tiles(8, 12)
    x_end = x_middle()
    arrived(z1_in)
    unpack(z1, yd1)
    near_middle = over_y(yd1, NEAR // 2, y1a, y1b)
    up_tiles(0, 3)
    near_end = near_middle()
    up_tiles(3, 5)
    xsum[...] = x_end().astype(bf16)
    far_middle = over_y(xsum, FAR // 2, y2a, y2b)
    up_tiles(5, 8)
    far_end = far_middle()
    up_tiles(8, 12)
    gi_ref[:, lo] = near_end().astype(bf16)
    gi_ref[:, hi] = far_end().astype(bf16)
    for copy in sent[-SEND_SEMS:]:
        copy.wait_send()
    pltpu.make_async_copy(up, gup_hbm.at[0], osem.at[0]).wait()
    pltpu.make_async_copy(down, gdown_hbm.at[0], osem.at[1]).wait()


def on_device(layer_input, grad_output, expert_ids, gate_probs, up_weight, down_weight):
    vmem = pl.BlockSpec(memory_space=pltpu.VMEM)
    hbm = pl.BlockSpec(memory_space=pl.ANY)

    def buf(*shape):
        return pltpu.VMEM(shape, bf16)

    return pl.pallas_call(
        kernel,
        out_shape=(
            jax.ShapeDtypeStruct((TOK, QUARTER), bf16),
            jax.ShapeDtypeStruct(up_weight.shape, bf16),
            jax.ShapeDtypeStruct(down_weight.shape, bf16),
        ),
        in_specs=[vmem, vmem, vmem, vmem, hbm, hbm],
        out_specs=(vmem, hbm, hbm),
        scratch_shapes=[
            buf(ROWS, D),
            buf(ROWS, D),
            buf(D, F),
            buf(F, D),
            buf(ROWS, F),
            buf(ROWS, F),
            pltpu.VMEM((4, 8, TOK), f32),
            buf(4 * BLOCK, 4 * TOK),
            buf(4 * TOK, NEAR),
            buf(4 * TOK, NEAR),
            buf(4 * TOK, ALL_FAR),
            buf(4 * TOK, ALL_FAR),
            buf(4 * BLOCK, NEAR),
            buf(4 * BLOCK, NEAR),
            buf(4 * BLOCK, ALL_FAR),
            buf(4 * BLOCK, ALL_FAR),
            buf(ROWS, D),
            buf(4, BLOCK, D),
            buf(4, 2, BLOCK, NEAR // 2),
            buf(4, 2, BLOCK, NEAR),
            buf(4 * BLOCK, NEAR),
            buf(4 * BLOCK, ALL_FAR),
            buf(4 * TOK, NEAR),
            buf(4 * TOK, ALL_FAR),
            buf(2, TOK, NEAR // 2),
            buf(2, TOK, NEAR),
            buf(2, TOK, FAR // 2),
            buf(2, TOK, FAR),
            buf(4 * TOK, FAR),
            buf(2, 4 * TOK, FAR // 2),
            buf(2, 4 * TOK, FAR),
            pltpu.SemaphoreType.DMA((SEND_SEMS,)),
            pltpu.SemaphoreType.DMA((N_SEMS,)),
            pltpu.SemaphoreType.DMA((2,)),
            pltpu.SemaphoreType.DMA((2,)),
        ],
        compiler_params=pltpu.CompilerParams(
            collective_id=0, has_side_effects=True, vmem_limit_bytes=63 * 1024 * 1024
        ),
    )(layer_input, grad_output, expert_ids.T, gate_probs.T, up_weight, down_weight)


def solution(mesh):
    return jax.shard_map(
        on_device,
        mesh=mesh,
        in_specs=(
            P(("dp", "expert"), "etp"),
            P(("dp", "expert"), "etp"),
            P(("dp", "expert"), None),
            P(("dp", "expert"), None),
            P("expert", None, ("dp", "etp")),
            P("expert", ("dp", "etp"), None),
        ),
        out_specs=(
            P(("dp", "expert"), "etp"),
            P("expert", None, ("dp", "etp")),
            P("expert", ("dp", "etp"), None),
        ),
        check_vma=False,
    )
```

```python
import jax
import jax.numpy as jnp
from jax import lax
from jax.experimental import pallas as pl
from jax.experimental.pallas import tpu as pltpu
from jax.sharding import PartitionSpec as P

inv_root_two = 0.7071067811865476
inv_root_tau = 0.3989422804014327
MESH = pl.DeviceIdType.MESH
bf16 = jnp.bfloat16
f32 = jnp.float32

TOK = 128
QUARTER = 768
NEAR = 512
FAR = 256
CAP = 36
BLOCK = 4 * CAP
CHUNK = 2 * BLOCK
ROWS = 4 * CHUNK
D = 3072
F = 1024
SPLIT = 4 * NEAR
ALL_FAR = 4 * FAR
TILE = 256
WIDE = 512
FAR_PARTS = (pl.ds(0, ALL_FAR // 2), pl.ds(ALL_FAR // 2, ALL_FAR // 2))
OFFSETS = (0, 3, 1, 2)
N_SEMS = 144
SEND_SEMS = 48


def pieces():
    out = []
    for k in range(4):
        out.append((k * NEAR, k * QUARTER, NEAR))
        out.append((SPLIT + k * FAR, k * QUARTER + NEAR, FAR))
    return out


def kernel(
    x_ref, g_ref, ids_ref, gates_ref, up_hbm, down_hbm,
    gi_ref, gup_ref, gdown_ref,
    rows_x, rows_g, hid, pre, meta, place,
    d1x, d1g, d2x, d2g, p1x, p1g, p2x, p2g,
    dx, r1, r2a, r2b, z1, z2, yd1, yd2, y1a, y1b, y2a, y2b, xsum, xa, xb,
    ssem, rsem, wsem,
):
    up, down = gup_ref.at[0], gdown_ref.at[0]
    dp = lax.axis_index("dp")
    ex = lax.axis_index("expert")
    x = lax.axis_index("etp")
    c = dp % 2
    yl = ex // 4
    z = ex % 4
    y = (dp // 2) * 2 + yl

    def device(x_, y_, z_, c_):
        return ((y_ // 2) * 2 + c_, (y_ % 2) * 4 + z_, x_)

    xp, xm, xo = (x + 1) % 4, (x + 3) % 4, (x + 2) % 4
    yp, ym, yo = (y + 1) % 4, (y + 3) % 4, (y + 2) % 4
    to_xp, to_xm = device(xp, y, z, c), device(xm, y, z, c)
    to_yp, to_ym = device(x, yp, z, c), device(x, ym, z, c)
    to_core = device(x, y, z, 1 - c)
    to_z = {d: device(x, y, (z + d) % 4, c) for d in (1, 2, 3)}

    def span(start, width):
        return pl.ds(pl.multiple_of(start, width), width)

    def tok(y_):
        return span(y_ * TOK, TOK)

    def packed(z_):
        return span(z_ * BLOCK, BLOCK)

    def block(z_, c_):
        return span((z_ * 2 + c_) * BLOCK, BLOCK)

    def chunk(z_):
        return span(z_ * CHUNK, CHUNK)

    def near(x_):
        return span(x_ * NEAR, NEAR)

    def far(x_):
        return span(x_ * FAR, FAR)

    all_near, all_far = slice(0, SPLIT), slice(SPLIT, D)
    sent = []

    def send(src, dst, to):
        i = len(sent)
        if i >= SEND_SEMS:
            sent[i - SEND_SEMS].wait_send()
        copy = pltpu.make_async_remote_copy(
            src_ref=src, dst_ref=dst, send_sem=ssem.at[i % SEND_SEMS], recv_sem=rsem.at[i],
            device_id=to, device_id_type=MESH,
        )
        copy.start()
        sent.append(copy)
        return copy

    def arrived(copies):
        for copy in copies:
            copy.wait_recv()

    def gather(own, into, below, here, above, down_to, up_to):
        one, two = into
        first = (
            send(own[0], one(here), up_to),
            send(own[1], two(here), down_to),
            send(own[0], one(here), down_to),
            send(own[1], two(here), up_to),
        )

        def forward():
            first[0].wait_recv()
            up = send(one(below), one(below), up_to)
            first[1].wait_recv()
            down = send(two(above), two(above), down_to)
            return (first[2], first[3], up, down)

        return forward

    def scatter(at, half, below, here, above, opposite, down_to, up_to, a, b):
        low, high = slice(0, half), slice(half, 2 * half)
        halves = (send(at(opposite, low), a.at[0], up_to), send(at(opposite, high), a.at[1], down_to))

        def middle():
            halves[0].wait_recv()
            ref = at(above, low)
            ref[...] = (ref[...].astype(f32) + a[0].astype(f32)).astype(bf16)
            up = send(at(above, None), b.at[0], up_to)
            halves[1].wait_recv()
            ref = at(below, high)
            ref[...] = (ref[...].astype(f32) + a[1].astype(f32)).astype(bf16)
            down = send(at(below, None), b.at[1], down_to)

            def end():
                arrived((up, down))
                return at(here, None)[...].astype(f32) + b[0].astype(f32) + b[1].astype(f32)

            return end

        return middle

    partners = (to_xp, to_xm, to_yp, to_ym, to_core, to_z[1], to_z[2], to_z[3])
    barrier = pltpu.get_barrier_semaphore()
    for partner in partners:
        pl.semaphore_signal(barrier, inc=1, device_id=partner, device_id_type=MESH)
    pl.semaphore_wait(barrier, len(partners))

    lo, hi = pl.ds(0, NEAR), pl.ds(NEAR, FAR)
    y1_forward = gather(
        (x_ref.at[:, lo], g_ref.at[:, lo]),
        (lambda k: d1x.at[tok(k)], lambda k: d1g.at[tok(k)]),
        ym, y, yp, to_ym, to_yp,
    )
    x2_forward = gather(
        (x_ref.at[:, hi], g_ref.at[:, hi]),
        (lambda k: d2x.at[tok(y), far(k)], lambda k: d2g.at[tok(y), far(k)]),
        xm, x, xp, to_xm, to_xp,
    )
    for there, here, width in pieces():
        pltpu.make_async_copy(
            up_hbm.at[0, pl.ds(here, width), :], up.at[pl.ds(there, width), :], wsem.at[0]
        ).start()
        pltpu.make_async_copy(
            down_hbm.at[0, :, pl.ds(here, width)], down.at[:, pl.ds(there, width)], wsem.at[1]
        ).start()

    ids = ids_ref[...]
    expert = lax.broadcasted_iota(jnp.int32, (8, TOK), 0)
    one = jnp.where(expert == ids[0:1], 1.0, 0.0)
    two = jnp.where(expert == ids[1:2], 1.0, 0.0)
    earlier = (
        lax.broadcasted_iota(jnp.int32, (TOK, TOK), 0) < lax.broadcasted_iota(jnp.int32, (TOK, TOK), 1)
    )
    before = jnp.dot(
        jnp.concatenate([one, two], axis=0).astype(bf16),
        jnp.where(earlier, 1.0, 0.0).astype(bf16),
        preferred_element_type=f32,
    )
    one_at = jnp.sum(before[:8] * one, axis=0, keepdims=True)
    two_at = jnp.sum((before[8:] + jnp.sum(one, axis=1, keepdims=True)) * two, axis=0, keepdims=True)
    upper = ids >= 4
    base = (jnp.where(upper, ids - 4, ids) * BLOCK + y * CAP).astype(f32)
    for k, at in ((0, one_at), (1, two_at)):
        target = base[k:k + 1] + at
        meta[y, k:k + 1] = jnp.where(upper[k:k + 1], -1.0, target)
        meta[y, k + 2:k + 3] = jnp.where(upper[k:k + 1], target, -1.0)
        meta[y, k + 4:k + 5] = gates_ref[k:k + 1, :]
    meta[y, 6:8] = jnp.zeros((2, TOK), f32)
    m_p = send(meta.at[y], meta.at[y], to_yp)
    m_m = send(meta.at[y], meta.at[y], to_ym)
    d1x[tok(y), :] = x_ref[:, lo]
    d1g[tok(y), :] = g_ref[:, lo]
    d2x[tok(y), far(x)] = x_ref[:, hi]
    d2g[tok(y), far(x)] = g_ref[:, hi]

    x2_in = x2_forward()
    y1_in = y1_forward()
    m_p.wait_recv()
    m_f = send(meta.at[ym], meta.at[ym], to_yp)
    arrived(x2_in)

    def y2_gather(cols):
        return gather(
            (d2x.at[tok(y), cols], d2g.at[tok(y), cols]),
            (lambda k: d2x.at[tok(k), cols], lambda k: d2g.at[tok(k), cols]),
            ym, y, yp, to_ym, to_yp,
        )

    y2_forward = [y2_gather(FAR_PARTS[0])]
    arrived((m_m, m_f))
    row = lax.broadcasted_iota(jnp.int32, (4 * BLOCK, TOK), 0).astype(f32)
    gate = jnp.zeros((4 * BLOCK, 1), f32)
    for t in range(4):
        m = meta[t]
        first = row == jnp.where(yl == 0, m[0:1], m[2:3])
        second = row == jnp.where(yl == 0, m[1:2], m[3:4])
        hits = jnp.where(first, 1.0, 0.0) + jnp.where(second, 1.0, 0.0)
        place[:, t * TOK:(t + 1) * TOK] = hits.astype(bf16)
        gates = jnp.where(first, m[4:5], 0.0) + jnp.where(second, m[5:6], 0.0)
        gate = gate + jnp.sum(gates, axis=1, keepdims=True)

    def pack(from_x, from_g, to_x, to_g, cols):
        to_x[:, cols] = jnp.dot(place[...], from_x[:, cols], preferred_element_type=f32).astype(bf16)
        to_g[:, cols] = (
            jnp.dot(place[...], from_g[:, cols], preferred_element_type=f32) * gate
        ).astype(bf16)

    def to_expert(d, from_x, from_g, cols, into):
        there = (packed((z + d) % 4), cols)
        here = (block(z, c), into)
        return (
            send(from_x.at[there], rows_x.at[here], to_z[d]),
            send(from_g.at[there], rows_g.at[here], to_z[d]),
        )

    def keep(from_x, from_g, cols, into):
        here = (block(z, c), into)
        rows_x[here] = from_x[packed(z), cols]
        rows_g[here] = from_g[packed(z), cols]

    zs = [(z + o) % 4 for o in OFFSETS]
    x_in = {}
    near_z = {}
    far_z = {}
    near_in = {}
    far_in = {}
    r1_far = {}
    r1_near = {}
    r2_middle = {}
    r2_end = {}
    z1_in = []
    z2_in = []

    def x_send(j):
        if j > 0:
            arrived(near_z[(4 - OFFSETS[j]) % 4])
        rows = block(zs[j], c)
        x_in[j] = gather(
            (rows_x.at[rows, near(x)], rows_g.at[rows, near(x)]),
            (lambda k: rows_x.at[rows, near(k)], lambda k: rows_g.at[rows, near(k)]),
            xm, x, xp, to_xm, to_xp,
        )

    def x_forward(j):
        x_in[j] = x_in[j]()

    def near_send(j):
        arrived(x_in[j])
        at = (block(zs[j], c), all_near)
        near_in[j] = [send(r.at[at], r.at[at], to_core) for r in (rows_x, rows_g)]

    def far_part_send(j, part):
        at = (block(zs[j], c), pl.ds(SPLIT + part * (ALL_FAR // 2), ALL_FAR // 2))
        far_in[j] = far_in.get(j, []) + [send(r.at[at], r.at[at], to_core) for r in (rows_x, rows_g)]

    def far_send(j):
        if j > 0:
            arrived(far_z[(4 - OFFSETS[j]) % 4])
        at = (block(zs[j], c), all_far)
        far_in[j] = [send(r.at[at], r.at[at], to_core) for r in (rows_x, rows_g)]

    def hidden_of(j, first, last):
        if first == 0:
            arrived(near_in[j])
            arrived(far_in[j])
        rows = chunk(zs[j])

        @pl.loop(first, last)
        def _(n):
            cols = pl.ds(pl.multiple_of(n * WIDE, WIDE), WIDE)
            act = jnp.dot(rows_x[rows, :], up[:, cols], preferred_element_type=f32)
            back = lax.dot_general(
                rows_g[rows, :], down[cols, :], (((1,), (1,)), ((), ())),
                preferred_element_type=f32,
            )
            half_cdf = 0.5 * (1.0 + lax.erf(act * inv_root_two))
            hid[rows, cols] = (act * half_cdf).astype(bf16)
            slope = half_cdf + act * jnp.exp(-0.5 * act * act) * inv_root_tau
            pre[rows, cols] = (back * slope).astype(bf16)

    def input_grad(j, first, last):
        rows = chunk(zs[j])

        @pl.loop(first, last)
        def _(n):
            cols = pl.ds(pl.multiple_of(n * F, F), F)
            dx[rows, cols] = lax.dot_general(
                pre[rows, :], up[cols, :], (((1,), (1,)), ((), ())),
                preferred_element_type=f32,
            ).astype(bf16)

    def input_grad_of(j):
        input_grad(j, SPLIT // F, D // F)
        r1_far[j] = send(dx.at[block(zs[j], 1 - c), all_far], r1.at[j, :, all_far], to_core)
        input_grad(j, 0, SPLIT // F)
        r1_near[j] = send(dx.at[block(zs[j], 1 - c), all_near], r1.at[j, :, all_near], to_core)

    def add_core(j):
        rows = block(zs[j], c)
        r1_far[j].wait_recv()
        total = (dx[rows, all_far].astype(f32) + r1[j, :, all_far].astype(f32)).astype(bf16)
        if OFFSETS[j] == 0:
            z2[packed(z), :] = total
        else:
            dx[rows, all_far] = total
            z2_in.append(send(dx.at[rows, all_far], z2.at[packed(z)], to_z[OFFSETS[j]]))
        r1_near[j].wait_recv()
        dx[rows, all_near] = (
            dx[rows, all_near].astype(f32) + r1[j, :, all_near].astype(f32)
        ).astype(bf16)

        def at(k, half):
            if half is None:
                return dx.at[rows, near(k)]
            return dx.at[rows, span(k * NEAR + half.start, NEAR // 2)]

        r2_middle[j] = scatter(at, NEAR // 2, xm, x, xp, xo, to_xm, to_xp, r2a.at[j], r2b.at[j])

    def add_far(j):
        r2_end[j] = r2_middle[j]()

    def add_near(j):
        rows = block(zs[j], c)
        total = r2_end[j]().astype(bf16)
        if OFFSETS[j] == 0:
            z1[packed(z), :] = total
        else:
            dx[rows, near(x)] = total
            z1_in.append(send(dx.at[rows, near(x)], z1.at[packed(z)], to_z[OFFSETS[j]]))

    def unpack(rows, tokens):
        tokens[...] = lax.dot_general(
            place[...], rows[...], (((0,), (0,)), ((), ())), preferred_element_type=f32
        ).astype(bf16)

    def over_x(tokens, a, b):
        def at(k, part):
            return tokens.at[:, far(k)] if part is None else tokens.at[:, span(k * FAR + part.start, FAR // 2)]

        return scatter(at, FAR // 2, xm, x, xp, xo, to_xm, to_xp, a, b)

    def over_y(tokens, half, a, b):
        def at(k, part):
            return tokens.at[tok(k)] if part is None else tokens.at[tok(k), part]

        return scatter(at, half, ym, y, yp, yo, to_ym, to_yp, a, b)

    def down_tiles(k, first, last):
        wide = slice(k * F, (k + 1) * F)

        @pl.loop(first, last)
        def _(n):
            cols = pl.ds(pl.multiple_of(n * TILE, TILE), TILE)
            part = lax.dot_general(
                hid[:, cols], rows_g[:, wide], (((0,), (0,)), ((), ())),
                preferred_element_type=f32,
            ).astype(bf16)
            for there, here, width in pieces():
                if wide.start <= there < wide.stop:
                    start = there - wide.start
                    down[cols, pl.ds(here, width)] = part[:, start:start + width]

    def up_tiles(first, last):
        @pl.loop(first, last)
        def _(n):
            cols = pl.ds(pl.multiple_of(n * TILE, TILE), TILE)
            if last * TILE <= SPLIT:
                here = n // 2 * QUARTER + n % 2 * TILE
            else:
                here = (n - SPLIT // TILE) * QUARTER + NEAR
            up[pl.ds(pl.multiple_of(here, TILE), TILE), :] = lax.dot_general(
                rows_x[:, cols], pre[...], (((0,), (0,)), ((), ())),
                preferred_element_type=f32,
            ).astype(bf16)

    def near_to(d):
        near_z[d] = to_expert(d, p1x, p1g, pl.ds(0, NEAR), near(x))

    def far_to(d, part):
        into = pl.ds(SPLIT + part * (ALL_FAR // 2), ALL_FAR // 2)
        far_z[d] = far_z.get(d, ()) + to_expert(d, p2x, p2g, FAR_PARTS[part], into)

    def far_pack(part):
        pack(d2x, d2g, p2x, p2g, FAR_PARTS[part])
        far_to(1, part)
        far_to(3, part)
        keep(p2x, p2g, FAR_PARTS[part], pl.ds(SPLIT + part * (ALL_FAR // 2), ALL_FAR // 2))

    arrived(y1_in)
    pack(d1x, d1g, p1x, p1g, pl.ds(0, NEAR))
    near_to(1)
    near_to(3)
    keep(p1x, p1g, pl.ds(0, NEAR), near(x))
    x_send(0)
    y2_first = y2_forward[0]()
    y2_second = y2_gather(FAR_PARTS[1])
    x_forward(0)
    arrived(y2_first)
    far_pack(0)
    far_part_send(0, 0)
    x_send(1)
    near_to(2)
    y2_second = y2_second()
    x_send(2)
    near_send(0)
    arrived(y2_second)
    far_pack(1)
    far_part_send(0, 1)
    far_to(2, 0)
    far_to(2, 1)
    x_forward(1)
    x_send(3)
    pltpu.make_async_copy(up_hbm.at[0], up, wsem.at[0]).wait()
    pltpu.make_async_copy(down_hbm.at[0], down, wsem.at[1]).wait()
    hidden_of(0, 0, 2)
    near_send(1)
    x_forward(2)
    input_grad_of(0)
    far_send(1)
    hidden_of(1, 0, 1)
    add_core(0)
    x_forward(3)
    near_send(2)
    hidden_of(1, 1, 2)
    far_send(2)
    input_grad_of(1)
    add_far(0)
    near_send(3)
    hidden_of(2, 0, 1)
    add_core(1)
    hidden_of(2, 1, 2)
    far_send(3)
    add_near(0)
    input_grad_of(2)
    add_far(1)
    hidden_of(3, 0, 1)
    add_core(2)
    add_near(1)
    hidden_of(3, 1, 2)
    add_far(2)
    input_grad_of(3)
    add_near(2)
    down_tiles(0, 0, 2)
    add_core(3)
    down_tiles(0, 2, 4)
    down_tiles(1, 0, 1)
    add_far(3)
    down_tiles(1, 1, 4)
    add_near(3)
    arrived(z2_in)
    unpack(z2, yd2)
    x_middle = over_x(yd2, xa, xb)
    down_tiles(2, 0, 4)
    x_end = x_middle()
    arrived(z1_in)
    unpack(z1, yd1)
    near_middle = over_y(yd1, NEAR // 2, y1a, y1b)
    up_tiles(0, 3)
    near_end = near_middle()
    up_tiles(3, 5)
    xsum[...] = x_end().astype(bf16)
    far_middle = over_y(xsum, FAR // 2, y2a, y2b)
    up_tiles(5, 8)
    far_end = far_middle()
    up_tiles(8, 12)
    gi_ref[:, lo] = near_end().astype(bf16)
    gi_ref[:, hi] = far_end().astype(bf16)
    for copy in sent[-SEND_SEMS:]:
        copy.wait_send()


def on_device(layer_input, grad_output, expert_ids, gate_probs, up_weight, down_weight):
    vmem = pl.BlockSpec(memory_space=pltpu.VMEM)
    hbm = pl.BlockSpec(memory_space=pl.ANY)

    def buf(*shape):
        return pltpu.VMEM(shape, bf16)

    return pl.pallas_call(
        kernel,
        out_shape=(
            jax.ShapeDtypeStruct((TOK, QUARTER), bf16),
            pltpu.VMEM(up_weight.shape, bf16),
            pltpu.VMEM(down_weight.shape, bf16),
        ),
        in_specs=[vmem, vmem, vmem, vmem, hbm, hbm],
        out_specs=(vmem, vmem, vmem),
        scratch_shapes=[
            buf(ROWS, D),
            buf(ROWS, D),
            buf(ROWS, F),
            buf(ROWS, F),
            pltpu.VMEM((4, 8, TOK), f32),
            buf(4 * BLOCK, 4 * TOK),
            buf(4 * TOK, NEAR),
            buf(4 * TOK, NEAR),
            buf(4 * TOK, ALL_FAR),
            buf(4 * TOK, ALL_FAR),
            buf(4 * BLOCK, NEAR),
            buf(4 * BLOCK, NEAR),
            buf(4 * BLOCK, ALL_FAR),
            buf(4 * BLOCK, ALL_FAR),
            buf(ROWS, D),
            buf(4, BLOCK, D),
            buf(4, 2, BLOCK, NEAR // 2),
            buf(4, 2, BLOCK, NEAR),
            buf(4 * BLOCK, NEAR),
            buf(4 * BLOCK, ALL_FAR),
            buf(4 * TOK, NEAR),
            buf(4 * TOK, ALL_FAR),
            buf(2, TOK, NEAR // 2),
            buf(2, TOK, NEAR),
            buf(2, TOK, FAR // 2),
            buf(2, TOK, FAR),
            buf(4 * TOK, FAR),
            buf(2, 4 * TOK, FAR // 2),
            buf(2, 4 * TOK, FAR),
            pltpu.SemaphoreType.DMA((SEND_SEMS,)),
            pltpu.SemaphoreType.DMA((N_SEMS,)),
            pltpu.SemaphoreType.DMA((2,)),
        ],
        compiler_params=pltpu.CompilerParams(
            collective_id=0, has_side_effects=True, vmem_limit_bytes=51 * 1024 * 1024
        ),
    )(layer_input, grad_output, expert_ids.T, gate_probs.T, up_weight, down_weight)


def solution(mesh):
    return jax.shard_map(
        on_device,
        mesh=mesh,
        in_specs=(
            P(("dp", "expert"), "etp"),
            P(("dp", "expert"), "etp"),
            P(("dp", "expert"), None),
            P(("dp", "expert"), None),
            P("expert", None, ("dp", "etp")),
            P("expert", ("dp", "etp"), None),
        ),
        out_specs=(
            P(("dp", "expert"), "etp"),
            P("expert", None, ("dp", "etp")),
            P("expert", ("dp", "etp"), None),
        ),
        check_vma=False,
    )
```

```python
import jax
import jax.numpy as jnp
from jax import lax
from jax.experimental import pallas as pl
from jax.experimental.pallas import tpu as pltpu
from jax.sharding import PartitionSpec as P

inv_root_two = 0.7071067811865476
inv_root_tau = 0.3989422804014327
MESH = pl.DeviceIdType.MESH
bf16 = jnp.bfloat16
f32 = jnp.float32

TOK = 128
QUARTER = 768
NEAR = 512
FAR = 256
CAP = 36
BLOCK = 4 * CAP
CHUNK = 2 * BLOCK
ROWS = 4 * CHUNK
D = 3072
F = 1024
SPLIT = 4 * NEAR
ALL_FAR = 4 * FAR
TILE = 256
WIDE = 512
FAR_PARTS = (pl.ds(0, ALL_FAR // 2), pl.ds(ALL_FAR // 2, ALL_FAR // 2))
OFFSETS = (0, 3, 1, 2)
N_SEMS = 144
SEND_SEMS = 48


def pieces():
    out = []
    for k in range(4):
        out.append((k * NEAR, k * QUARTER, NEAR))
        out.append((SPLIT + k * FAR, k * QUARTER + NEAR, FAR))
    return out


def kernel(
    x_ref, g_ref, ids_ref, gates_ref, up_hbm, down_hbm,
    gi_ref, gup_ref, gdown_ref,
    rows_x, rows_g, hid, pre, meta, place,
    d1x, d1g, d2x, d2g, p1x, p1g, p2x, p2g,
    dx, r1, r2a, r2b, z1, z2, yd1, yd2, y1a, y1b, y2a, y2b, xsum, xa, xb,
    ssem, rsem, wsem,
):
    up, down = gup_ref.at[0], gdown_ref.at[0]
    dp = lax.axis_index("dp")
    ex = lax.axis_index("expert")
    x = lax.axis_index("etp")
    c = dp % 2
    yl = ex // 4
    z = ex % 4
    y = (dp // 2) * 2 + yl

    def device(x_, y_, z_, c_):
        return ((y_ // 2) * 2 + c_, (y_ % 2) * 4 + z_, x_)

    xp, xm, xo = (x + 1) % 4, (x + 3) % 4, (x + 2) % 4
    yp, ym, yo = (y + 1) % 4, (y + 3) % 4, (y + 2) % 4
    to_xp, to_xm = device(xp, y, z, c), device(xm, y, z, c)
    to_yp, to_ym = device(x, yp, z, c), device(x, ym, z, c)
    to_core = device(x, y, z, 1 - c)
    to_z = {d: device(x, y, (z + d) % 4, c) for d in (1, 2, 3)}

    def span(start, width):
        return pl.ds(pl.multiple_of(start, width), width)

    def tok(y_):
        return span(y_ * TOK, TOK)

    def packed(z_):
        return span(z_ * BLOCK, BLOCK)

    def block(z_, c_):
        return span((z_ * 2 + c_) * BLOCK, BLOCK)

    def chunk(z_):
        return span(z_ * CHUNK, CHUNK)

    def near(x_):
        return span(x_ * NEAR, NEAR)

    def far(x_):
        return span(x_ * FAR, FAR)

    all_near, all_far = slice(0, SPLIT), slice(SPLIT, D)
    sent = []

    def send(src, dst, to):
        i = len(sent)
        if i >= SEND_SEMS:
            sent[i - SEND_SEMS].wait_send()
        copy = pltpu.make_async_remote_copy(
            src_ref=src, dst_ref=dst, send_sem=ssem.at[i % SEND_SEMS], recv_sem=rsem.at[i],
            device_id=to, device_id_type=MESH,
        )
        copy.start()
        sent.append(copy)
        return copy

    def arrived(copies):
        for copy in copies:
            copy.wait_recv()

    def gather(own, into, below, here, above, down_to, up_to):
        one, two = into
        first = (
            send(own[0], one(here), up_to),
            send(own[1], two(here), down_to),
            send(own[0], one(here), down_to),
            send(own[1], two(here), up_to),
        )

        def forward():
            first[0].wait_recv()
            up = send(one(below), one(below), up_to)
            first[1].wait_recv()
            down = send(two(above), two(above), down_to)
            return (first[2], first[3], up, down)

        return forward

    def scatter(at, half, below, here, above, opposite, down_to, up_to, a, b):
        low, high = slice(0, half), slice(half, 2 * half)
        halves = (send(at(opposite, low), a.at[0], up_to), send(at(opposite, high), a.at[1], down_to))

        def middle():
            halves[0].wait_recv()
            ref = at(above, low)
            ref[...] = (ref[...].astype(f32) + a[0].astype(f32)).astype(bf16)
            up = send(at(above, None), b.at[0], up_to)
            halves[1].wait_recv()
            ref = at(below, high)
            ref[...] = (ref[...].astype(f32) + a[1].astype(f32)).astype(bf16)
            down = send(at(below, None), b.at[1], down_to)

            def end():
                arrived((up, down))
                return at(here, None)[...].astype(f32) + b[0].astype(f32) + b[1].astype(f32)

            return end

        return middle

    partners = (to_xp, to_xm, to_yp, to_ym, to_core, to_z[1], to_z[2], to_z[3])
    barrier = pltpu.get_barrier_semaphore()
    for partner in partners:
        pl.semaphore_signal(barrier, inc=1, device_id=partner, device_id_type=MESH)
    pl.semaphore_wait(barrier, len(partners))

    lo, hi = pl.ds(0, NEAR), pl.ds(NEAR, FAR)
    y1_forward = gather(
        (x_ref.at[:, lo], g_ref.at[:, lo]),
        (lambda k: d1x.at[tok(k)], lambda k: d1g.at[tok(k)]),
        ym, y, yp, to_ym, to_yp,
    )
    x2_forward = gather(
        (x_ref.at[:, hi], g_ref.at[:, hi]),
        (lambda k: d2x.at[tok(y), far(k)], lambda k: d2g.at[tok(y), far(k)]),
        xm, x, xp, to_xm, to_xp,
    )
    for there, here, width in pieces():
        pltpu.make_async_copy(
            up_hbm.at[0, pl.ds(here, width), :], up.at[pl.ds(there, width), :], wsem.at[0]
        ).start()
        pltpu.make_async_copy(
            down_hbm.at[0, :, pl.ds(here, width)], down.at[:, pl.ds(there, width)], wsem.at[1]
        ).start()

    ids = ids_ref[...]
    expert = lax.broadcasted_iota(jnp.int32, (8, TOK), 0)
    one = jnp.where(expert == ids[0:1], 1.0, 0.0)
    two = jnp.where(expert == ids[1:2], 1.0, 0.0)
    earlier = (
        lax.broadcasted_iota(jnp.int32, (TOK, TOK), 0) < lax.broadcasted_iota(jnp.int32, (TOK, TOK), 1)
    )
    before = jnp.dot(
        jnp.concatenate([one, two], axis=0).astype(bf16),
        jnp.where(earlier, 1.0, 0.0).astype(bf16),
        preferred_element_type=f32,
    )
    one_at = jnp.sum(before[:8] * one, axis=0, keepdims=True)
    two_at = jnp.sum((before[8:] + jnp.sum(one, axis=1, keepdims=True)) * two, axis=0, keepdims=True)
    upper = ids >= 4
    base = (jnp.where(upper, ids - 4, ids) * BLOCK + y * CAP).astype(f32)
    for k, at in ((0, one_at), (1, two_at)):
        target = base[k:k + 1] + at
        meta[y, k:k + 1] = jnp.where(upper[k:k + 1], -1.0, target)
        meta[y, k + 2:k + 3] = jnp.where(upper[k:k + 1], target, -1.0)
        meta[y, k + 4:k + 5] = gates_ref[k:k + 1, :]
    meta[y, 6:8] = jnp.zeros((2, TOK), f32)
    m_p = send(meta.at[y], meta.at[y], to_yp)
    m_m = send(meta.at[y], meta.at[y], to_ym)
    d1x[tok(y), :] = x_ref[:, lo]
    d1g[tok(y), :] = g_ref[:, lo]
    d2x[tok(y), far(x)] = x_ref[:, hi]
    d2g[tok(y), far(x)] = g_ref[:, hi]

    x2_in = x2_forward()
    y1_in = y1_forward()
    m_p.wait_recv()
    m_f = send(meta.at[ym], meta.at[ym], to_yp)
    arrived(x2_in)

    def y2_gather(cols):
        return gather(
            (d2x.at[tok(y), cols], d2g.at[tok(y), cols]),
            (lambda k: d2x.at[tok(k), cols], lambda k: d2g.at[tok(k), cols]),
            ym, y, yp, to_ym, to_yp,
        )

    y2_forward = [y2_gather(FAR_PARTS[0])]
    arrived((m_m, m_f))
    row = lax.broadcasted_iota(jnp.int32, (4 * BLOCK, TOK), 0).astype(f32)
    gate = jnp.zeros((4 * BLOCK, 1), f32)
    for t in range(4):
        m = meta[t]
        first = row == jnp.where(yl == 0, m[0:1], m[2:3])
        second = row == jnp.where(yl == 0, m[1:2], m[3:4])
        hits = jnp.where(first, 1.0, 0.0) + jnp.where(second, 1.0, 0.0)
        place[:, t * TOK:(t + 1) * TOK] = hits.astype(bf16)
        gates = jnp.where(first, m[4:5], 0.0) + jnp.where(second, m[5:6], 0.0)
        gate = gate + jnp.sum(gates, axis=1, keepdims=True)

    def pack(from_x, from_g, to_x, to_g, cols):
        to_x[:, cols] = jnp.dot(place[...], from_x[:, cols], preferred_element_type=f32).astype(bf16)
        to_g[:, cols] = (
            jnp.dot(place[...], from_g[:, cols], preferred_element_type=f32) * gate
        ).astype(bf16)

    def to_expert(d, from_x, from_g, cols, into):
        there = (packed((z + d) % 4), cols)
        here = (block(z, c), into)
        return (
            send(from_x.at[there], rows_x.at[here], to_z[d]),
            send(from_g.at[there], rows_g.at[here], to_z[d]),
        )

    def keep(from_x, from_g, cols, into):
        here = (block(z, c), into)
        rows_x[here] = from_x[packed(z), cols]
        rows_g[here] = from_g[packed(z), cols]

    zs = [(z + o) % 4 for o in OFFSETS]
    x_in = {}
    near_z = {}
    far_z = {}
    near_in = {}
    far_in = {}
    r1_far = {}
    r1_near = {}
    r2_middle = {}
    r2_end = {}
    z1_in = []
    z2_in = []

    def x_send(j):
        if j > 0:
            arrived(near_z[(4 - OFFSETS[j]) % 4])
        rows = block(zs[j], c)
        x_in[j] = gather(
            (rows_x.at[rows, near(x)], rows_g.at[rows, near(x)]),
            (lambda k: rows_x.at[rows, near(k)], lambda k: rows_g.at[rows, near(k)]),
            xm, x, xp, to_xm, to_xp,
        )

    def x_forward(j):
        x_in[j] = x_in[j]()

    def near_send(j):
        arrived(x_in[j])
        at = (block(zs[j], c), all_near)
        near_in[j] = [send(r.at[at], r.at[at], to_core) for r in (rows_x, rows_g)]

    def far_part_send(j, part):
        at = (block(zs[j], c), pl.ds(SPLIT + part * (ALL_FAR // 2), ALL_FAR // 2))
        far_in[j] = far_in.get(j, []) + [send(r.at[at], r.at[at], to_core) for r in (rows_x, rows_g)]

    def far_send(j):
        if j > 0:
            arrived(far_z[(4 - OFFSETS[j]) % 4])
        at = (block(zs[j], c), all_far)
        far_in[j] = [send(r.at[at], r.at[at], to_core) for r in (rows_x, rows_g)]

    def hidden_of(j, first, last):
        if first == 0:
            arrived(near_in[j])
            arrived(far_in[j])
        rows = chunk(zs[j])

        @pl.loop(first, last)
        def _(n):
            cols = pl.ds(pl.multiple_of(n * WIDE, WIDE), WIDE)
            act = jnp.dot(rows_x[rows, :], up[:, cols], preferred_element_type=f32)
            back = lax.dot_general(
                rows_g[rows, :], down[cols, :], (((1,), (1,)), ((), ())),
                preferred_element_type=f32,
            )
            half_cdf = 0.5 * (1.0 + lax.erf(act * inv_root_two))
            hid[rows, cols] = (act * half_cdf).astype(bf16)
            slope = half_cdf + act * jnp.exp(-0.5 * act * act) * inv_root_tau
            pre[rows, cols] = (back * slope).astype(bf16)

    def input_grad(j, first, last):
        rows = chunk(zs[j])

        @pl.loop(first, last)
        def _(n):
            cols = pl.ds(pl.multiple_of(n * F, F), F)
            dx[rows, cols] = lax.dot_general(
                pre[rows, :], up[cols, :], (((1,), (1,)), ((), ())),
                preferred_element_type=f32,
            ).astype(bf16)

    def input_grad_of(j):
        input_grad(j, SPLIT // F, D // F)
        r1_far[j] = send(dx.at[block(zs[j], 1 - c), all_far], r1.at[j, :, all_far], to_core)
        input_grad(j, 0, SPLIT // F)
        r1_near[j] = send(dx.at[block(zs[j], 1 - c), all_near], r1.at[j, :, all_near], to_core)

    def add_core(j):
        rows = block(zs[j], c)
        r1_far[j].wait_recv()
        total = (dx[rows, all_far].astype(f32) + r1[j, :, all_far].astype(f32)).astype(bf16)
        if OFFSETS[j] == 0:
            z2[packed(z), :] = total
        else:
            dx[rows, all_far] = total
            z2_in.append(send(dx.at[rows, all_far], z2.at[packed(z)], to_z[OFFSETS[j]]))
        r1_near[j].wait_recv()
        dx[rows, all_near] = (
            dx[rows, all_near].astype(f32) + r1[j, :, all_near].astype(f32)
        ).astype(bf16)

        def at(k, half):
            if half is None:
                return dx.at[rows, near(k)]
            return dx.at[rows, span(k * NEAR + half.start, NEAR // 2)]

        r2_middle[j] = scatter(at, NEAR // 2, xm, x, xp, xo, to_xm, to_xp, r2a.at[j], r2b.at[j])

    def add_far(j):
        r2_end[j] = r2_middle[j]()

    def add_near(j):
        rows = block(zs[j], c)
        total = r2_end[j]().astype(bf16)
        if OFFSETS[j] == 0:
            z1[packed(z), :] = total
        else:
            dx[rows, near(x)] = total
            z1_in.append(send(dx.at[rows, near(x)], z1.at[packed(z)], to_z[OFFSETS[j]]))

    def unpack(rows, tokens):
        tokens[...] = lax.dot_general(
            place[...], rows[...], (((0,), (0,)), ((), ())), preferred_element_type=f32
        ).astype(bf16)

    def over_x(tokens, a, b):
        def at(k, part):
            return tokens.at[:, far(k)] if part is None else tokens.at[:, span(k * FAR + part.start, FAR // 2)]

        return scatter(at, FAR // 2, xm, x, xp, xo, to_xm, to_xp, a, b)

    def over_y(tokens, half, a, b):
        def at(k, part):
            return tokens.at[tok(k)] if part is None else tokens.at[tok(k), part]

        return scatter(at, half, ym, y, yp, yo, to_ym, to_yp, a, b)

    def down_tiles(k, first, last):
        wide = slice(k * F, (k + 1) * F)

        @pl.loop(first, last)
        def _(n):
            cols = pl.ds(pl.multiple_of(n * TILE, TILE), TILE)
            part = lax.dot_general(
                hid[:, cols], rows_g[:, wide], (((0,), (0,)), ((), ())),
                preferred_element_type=f32,
            ).astype(bf16)
            for there, here, width in pieces():
                if wide.start <= there < wide.stop:
                    start = there - wide.start
                    down[cols, pl.ds(here, width)] = part[:, start:start + width]

    def up_tiles(first, last):
        @pl.loop(first, last)
        def _(n):
            cols = pl.ds(pl.multiple_of(n * TILE, TILE), TILE)
            if last * TILE <= SPLIT:
                here = n // 2 * QUARTER + n % 2 * TILE
            else:
                here = (n - SPLIT // TILE) * QUARTER + NEAR
            up[pl.ds(pl.multiple_of(here, TILE), TILE), :] = lax.dot_general(
                rows_x[:, cols], pre[...], (((0,), (0,)), ((), ())),
                preferred_element_type=f32,
            ).astype(bf16)

    def near_to(d):
        near_z[d] = to_expert(d, p1x, p1g, pl.ds(0, NEAR), near(x))

    def far_to(d, part):
        into = pl.ds(SPLIT + part * (ALL_FAR // 2), ALL_FAR // 2)
        far_z[d] = far_z.get(d, ()) + to_expert(d, p2x, p2g, FAR_PARTS[part], into)

    def far_pack(part):
        pack(d2x, d2g, p2x, p2g, FAR_PARTS[part])
        far_to(1, part)
        far_to(3, part)
        keep(p2x, p2g, FAR_PARTS[part], pl.ds(SPLIT + part * (ALL_FAR // 2), ALL_FAR // 2))

    arrived(y1_in)
    pack(d1x, d1g, p1x, p1g, pl.ds(0, NEAR))
    near_to(1)
    near_to(3)
    keep(p1x, p1g, pl.ds(0, NEAR), near(x))
    x_send(0)
    y2_first = y2_forward[0]()
    y2_second = y2_gather(FAR_PARTS[1])
    x_forward(0)
    arrived(y2_first)
    far_pack(0)
    far_part_send(0, 0)
    x_send(1)
    near_to(2)
    y2_second = y2_second()
    x_send(2)
    near_send(0)
    arrived(y2_second)
    far_pack(1)
    far_part_send(0, 1)
    far_to(2, 0)
    far_to(2, 1)
    x_forward(1)
    x_send(3)
    pltpu.make_async_copy(up_hbm.at[0], up, wsem.at[0]).wait()
    pltpu.make_async_copy(down_hbm.at[0], down, wsem.at[1]).wait()
    hidden_of(0, 0, 2)
    near_send(1)
    x_forward(2)
    input_grad_of(0)
    far_send(1)
    hidden_of(1, 0, 1)
    add_core(0)
    x_forward(3)
    near_send(2)
    hidden_of(1, 1, 2)
    far_send(2)
    input_grad_of(1)
    add_far(0)
    near_send(3)
    hidden_of(2, 0, 1)
    add_core(1)
    hidden_of(2, 1, 2)
    far_send(3)
    add_near(0)
    input_grad_of(2)
    add_far(1)
    hidden_of(3, 0, 1)
    add_core(2)
    add_near(1)
    hidden_of(3, 1, 2)
    add_far(2)
    input_grad_of(3)
    add_core(3)
    add_near(2)
    down_tiles(0, 0, 4)
    add_far(3)
    down_tiles(1, 0, 4)
    add_near(3)
    arrived(z2_in)
    unpack(z2, yd2)
    x_middle = over_x(yd2, xa, xb)
    down_tiles(2, 0, 4)
    x_end = x_middle()
    arrived(z1_in)
    unpack(z1, yd1)
    near_middle = over_y(yd1, NEAR // 2, y1a, y1b)
    up_tiles(0, 3)
    near_end = near_middle()
    up_tiles(3, 5)
    xsum[...] = x_end().astype(bf16)
    far_middle = over_y(xsum, FAR // 2, y2a, y2b)
    up_tiles(5, 8)
    far_end = far_middle()
    up_tiles(8, 12)
    gi_ref[:, lo] = near_end().astype(bf16)
    gi_ref[:, hi] = far_end().astype(bf16)
    for copy in sent[-SEND_SEMS:]:
        copy.wait_send()


def on_device(layer_input, grad_output, expert_ids, gate_probs, up_weight, down_weight):
    vmem = pl.BlockSpec(memory_space=pltpu.VMEM)
    hbm = pl.BlockSpec(memory_space=pl.ANY)

    def buf(*shape):
        return pltpu.VMEM(shape, bf16)

    return pl.pallas_call(
        kernel,
        out_shape=(
            jax.ShapeDtypeStruct((TOK, QUARTER), bf16),
            pltpu.VMEM(up_weight.shape, bf16),
            pltpu.VMEM(down_weight.shape, bf16),
        ),
        in_specs=[vmem, vmem, vmem, vmem, hbm, hbm],
        out_specs=(vmem, vmem, vmem),
        scratch_shapes=[
            buf(ROWS, D),
            buf(ROWS, D),
            buf(ROWS, F),
            buf(ROWS, F),
            pltpu.VMEM((4, 8, TOK), f32),
            buf(4 * BLOCK, 4 * TOK),
            buf(4 * TOK, NEAR),
            buf(4 * TOK, NEAR),
            buf(4 * TOK, ALL_FAR),
            buf(4 * TOK, ALL_FAR),
            buf(4 * BLOCK, NEAR),
            buf(4 * BLOCK, NEAR),
            buf(4 * BLOCK, ALL_FAR),
            buf(4 * BLOCK, ALL_FAR),
            buf(ROWS, D),
            buf(4, BLOCK, D),
            buf(4, 2, BLOCK, NEAR // 2),
            buf(4, 2, BLOCK, NEAR),
            buf(4 * BLOCK, NEAR),
            buf(4 * BLOCK, ALL_FAR),
            buf(4 * TOK, NEAR),
            buf(4 * TOK, ALL_FAR),
            buf(2, TOK, NEAR // 2),
            buf(2, TOK, NEAR),
            buf(2, TOK, FAR // 2),
            buf(2, TOK, FAR),
            buf(4 * TOK, FAR),
            buf(2, 4 * TOK, FAR // 2),
            buf(2, 4 * TOK, FAR),
            pltpu.SemaphoreType.DMA((SEND_SEMS,)),
            pltpu.SemaphoreType.DMA((N_SEMS,)),
            pltpu.SemaphoreType.DMA((2,)),
        ],
        compiler_params=pltpu.CompilerParams(
            collective_id=0, has_side_effects=True, vmem_limit_bytes=51 * 1024 * 1024
        ),
    )(layer_input, grad_output, expert_ids.T, gate_probs.T, up_weight, down_weight)


def solution(mesh):
    return jax.shard_map(
        on_device,
        mesh=mesh,
        in_specs=(
            P(("dp", "expert"), "etp"),
            P(("dp", "expert"), "etp"),
            P(("dp", "expert"), None),
            P(("dp", "expert"), None),
            P("expert", None, ("dp", "etp")),
            P("expert", ("dp", "etp"), None),
        ),
        out_specs=(
            P(("dp", "expert"), "etp"),
            P("expert", None, ("dp", "etp")),
            P("expert", ("dp", "etp"), None),
        ),
        check_vma=False,
    )
```
